32 devices in a mesh: groups: 2 (over x), ctx: 16 (over z, y, core).
Axes of the slice: x: 2, y: 2, z: 4, core: 2. Of those that a mesh axis runs over, the one named last changes fastest.
Arguments:
- receptance: bfloat16 [4096, 2048], P(('groups', 'ctx')), parts along dimension 0, may hold values from -6 to 6
- decay_logit: bfloat16 [4096, 2048], P(('groups', 'ctx')), parts along dimension 0, may hold values from -16 to 2
- token_keys: bfloat16 [4096, 2048], P(('groups', 'ctx')), parts along dimension 0, may hold values from -6 to 6
- token_values: bfloat16 [4096, 2048], P(('groups', 'ctx')), parts along dimension 0, may hold values from -6 to 6
- removal_key: bfloat16 [4096, 2048], P(('groups', 'ctx')), parts along dimension 0, may hold values from -6 to 6
- removal_rate: bfloat16 [4096, 2048], P(('groups', 'ctx')), parts along dimension 0, may hold values from 0 to 1
- output_grad: bfloat16 [4096, 2048], P(('groups', 'ctx')), parts along dimension 0, may hold values from -0.0390625 to 0.0390625
Outputs:
- grad_receptance: bfloat16 [4096, 2048], P(('groups', 'ctx')), parts along dimension 0
- grad_decay: bfloat16 [4096, 2048], P(('groups', 'ctx')), parts along dimension 0
- grad_keys: bfloat16 [4096, 2048], P(('groups', 'ctx')), parts along dimension 0
- grad_values: bfloat16 [4096, 2048], P(('groups', 'ctx')), parts along dimension 0
- grad_removal_key: bfloat16 [4096, 2048], P(('groups', 'ctx')), parts along dimension 0
- grad_removal_rate: bfloat16 [4096, 2048], P(('groups', 'ctx')), parts along dimension 0
The draws below stay inside these ranges and needn't reach their ends.
There are 2 independent parts, one for each index of `groups`. The reference program is written for one: setup_inputs(seed, part) draws one part's arguments, and reference() takes and returns one part's arrays. A program takes and returns all parts, laid end to end along the dimension named above; each array names one. Nothing has to cross between parts.
All inputs are finite; a program needn't handle non-finite values.
Results may differ from the reference program's by a relative error of at most 0.001.
Values sent between devices are 32-bit elements; how exact they have to be, the bound alone decides.
A program may use at most 448 MiB of HBM per device.

```python
import jax
import jax.numpy as jnp
from jax import lax

HEADS = 32
HS = 64
T_DEV = 128
SEQUENCE_TOKENS = 2048
WIDTH = 2048
N_CTX = 16


def head_classes(key, share):
    slow = jax.random.uniform(key, (HEADS,)) < share
    return jnp.repeat(slow, HS)


def draw_decay_logit(key, part):
    share = 0.5
    slow = head_classes(key, share)
    key = jax.random.fold_in(key, 11)
    key_vectors = jax.random.split(key, 6)
    channel_list = HEADS * HS
    spread = jnp.exp(jax.random.uniform(key_vectors[0], (channel_list,), jnp.float32, jnp.log(0.2), 0.0))
    rough = jnp.exp(jax.random.uniform(key_vectors[1], (SEQUENCE_TOKENS, channel_list), jnp.float32, jnp.log(0.5), jnp.log(2.0)))
    shard_factor = jnp.exp(jax.random.uniform(key_vectors[2], (SEQUENCE_TOKENS // T_DEV, 1, channel_list), jnp.float32, jnp.log(0.5), jnp.log(2.0)))
    shard_factor = jnp.broadcast_to(shard_factor, (SEQUENCE_TOKENS // T_DEV, T_DEV, channel_list)).reshape(SEQUENCE_TOKENS, channel_list)
    fast_rate = jax.random.uniform(key_vectors[3], (channel_list,), jnp.float32, 1.0 / 50.0, 1.0 / 30.0)
    rate_value = jnp.where(slow, spread / SEQUENCE_TOKENS, fast_rate)[None, :] * rough * shard_factor
    position_list = jax.random.randint(key_vectors[4], (2,), 0, SEQUENCE_TOKENS)
    token_run = jnp.any(jnp.arange(SEQUENCE_TOKENS)[:, None] == position_list[None, :], axis=1)
    token_run_rate = 0.6065306597126334 * jax.random.uniform(key_vectors[5], (SEQUENCE_TOKENS, channel_list), jnp.float32, 0.4, 0.8)
    rate_value = jnp.where(token_run[:, None], token_run_rate, rate_value)
    share_rate = rate_value / 0.6065306597126334
    logit = jnp.log(share_rate) - jnp.log1p(-share_rate)
    return logit.astype(jnp.bfloat16)


def draw_removal_rate(key, part):
    share = 0.5
    slow = head_classes(key, share)
    key = jax.random.fold_in(key, 23)
    key_vectors = jax.random.split(key, 2)
    channel_list = HEADS * HS
    small = jnp.exp(jax.random.uniform(key_vectors[0], (SEQUENCE_TOKENS, channel_list), jnp.float32, jnp.log(0.1), 0.0))
    large = jax.random.uniform(key_vectors[1], (SEQUENCE_TOKENS, channel_list), jnp.float32, 0.2, 1.0)
    rate_value = jnp.where(slow[None, :], small * (32.0 / SEQUENCE_TOKENS), large)
    return rate_value.astype(jnp.bfloat16)


def shard_levels(rng, shape, cuts, low, top_value):
    def one(axis_at, shards_of):
        heights = jax.random.uniform(jax.random.fold_in(jax.random.fold_in(rng, 6), axis_at), (shards_of,), jnp.float32, low / len(cuts), top_value / len(cuts))
        return jnp.repeat(jnp.exp(heights), shape[axis_at] // shards_of).reshape((-1,) + (1,) * (len(shape) - axis_at - 1))

    factor_of = one(*cuts[0])
    for cut in cuts[1:]:
        factor_of = factor_of * one(*cut)
    return factor_of


def normal_values(rng, extent, scale, bound, cuts=(), dtype=jnp.bfloat16):
    result = jax.random.normal(rng, extent, jnp.float32) * scale
    if len(cuts) > 0:
        result = shard_levels(rng, extent, cuts, -0.22, 0.18) * result
    return jnp.clip(result, min=-bound, max=bound).astype(dtype)


def setup_inputs(seed: int = 0, part: int = 0) -> dict:
    splits = jax.random.split(jax.random.key(seed), 8)
    part_keys = jax.random.split(jax.random.fold_in(splits[7], part), 8)
    return {
        "receptance": normal_values(part_keys[0], (SEQUENCE_TOKENS, WIDTH), 1.0, 6.0, ((0, 16),)),
        "decay_logit": draw_decay_logit(jax.random.fold_in(jax.random.fold_in(splits[7], part), 71), part),
        "token_keys": normal_values(part_keys[2], (SEQUENCE_TOKENS, WIDTH), 1.0, 6.0, ((0, 16),)),
        "token_values": normal_values(part_keys[3], (SEQUENCE_TOKENS, WIDTH), 1.0, 6.0, ((0, 16),)),
        "removal_key": normal_values(part_keys[4], (SEQUENCE_TOKENS, WIDTH), 1.0, 6.0, ((0, 16),)),
        "removal_rate": draw_removal_rate(jax.random.fold_in(jax.random.fold_in(splits[7], part), 71), part),
        "output_grad": normal_values(part_keys[6], (SEQUENCE_TOKENS, WIDTH), ((64 * SEQUENCE_TOKENS) ** -0.5), 0.0390625, ((0, 16),)),
    }


DECAY_SCALE = 0.6065306597126334
precise = lax.Precision.HIGHEST

def prepare(receptance, decay_logit, token_keys, token_values, removal_key, removal_rate):

    def headed(array):
        return array.astype(jnp.float32).reshape(array.shape[0], HEADS, HS)
    queries = headed(receptance)
    log_decay = -DECAY_SCALE * jax.nn.sigmoid(headed(decay_logit))
    direction = headed(removal_key)
    direction = direction * lax.rsqrt(lax.optimization_barrier(jnp.sum(direction * direction, axis=-1, keepdims=True)) + 1e-06)
    return (queries, log_decay, headed(token_keys), headed(token_values), -direction, direction * headed(removal_rate))

def token_step(state, pieces):
    queries, log_decay, key_rows, value_rows, take_dir, give_dir = pieces
    removed = jnp.einsum('hij,hj->hi', state, take_dir, precision=precise)
    state = state * jnp.exp(log_decay)[:, None, :] + removed[:, :, None] * give_dir[:, None, :] + value_rows[:, :, None] * key_rows[:, None, :]
    return (state, jnp.einsum('hij,hj->hi', state, queries, precision=precise))

def shard_pass(state, pieces):
    return lax.scan(token_step, state, pieces)

def layer(receptance, decay_logit, token_keys, token_values, removal_key, removal_rate):
    prepared = prepare(receptance, decay_logit, token_keys, token_values, removal_key, removal_rate)
    split = tuple((array.reshape(N_CTX, T_DEV, HEADS, HS) for array in prepared))
    initial = jnp.zeros((HEADS, HS, HS), jnp.float32)
    final, outputs = lax.scan(jax.checkpoint(shard_pass), initial, split)
    return outputs.reshape(SEQUENCE_TOKENS, HEADS, HS)

def reference(receptance, decay_logit, token_keys, token_values, removal_key, removal_rate, output_grad):
    outputs, pullback = jax.vjp(layer, receptance, decay_logit, token_keys, token_values, removal_key, removal_rate)
    grads = pullback(output_grad.astype(jnp.float32).reshape(SEQUENCE_TOKENS, HEADS, HS))
    return (grads[0].astype(jnp.bfloat16), grads[1].astype(jnp.bfloat16), grads[2].astype(jnp.bfloat16), grads[3].astype(jnp.bfloat16), grads[4].astype(jnp.bfloat16), grads[5].astype(jnp.bfloat16))
```

```python
import functools

import jax
import jax.numpy as jnp
from jax import lax
from jax.experimental import pallas as pl
from jax.experimental.pallas import tpu as pltpu
from jax.sharding import PartitionSpec as P

HS = 64
LANES = 128
ROWS = 128
DECAY_SCALE = 0.6065306597126334
MESH = pl.DeviceIdType.MESH
NN = (((1,), (0,)), ((), ()))
NT = (((1,), (1,)), ((), ()))
TN = (((0,), (0,)), ((), ()))
F32 = jnp.float32
BF16 = jnp.bfloat16


def dot(x, y, dims):
    return lax.dot_general(x, y, dims, preferred_element_type=F32)


def split(x):
    if x.dtype == BF16:
        return (x, None)
    high = x.astype(BF16)
    return (high, (x - high.astype(F32)).astype(BF16))


def mm(x, y, dims=NN):
    total = dot(x[0], y[0], dims)
    if y[1] is not None:
        total = total + dot(x[0], y[1], dims)
    if x[1] is not None:
        total = total + dot(x[1], y[0], dims)
    return total


def masked(x, mask):
    return tuple(None if part is None else part * mask for part in x)


def stack(x, y):
    low = None
    if x[1] is not None or y[1] is not None:
        low = jnp.concatenate(
            [jnp.zeros_like(z[0]) if z[1] is None else z[1] for z in (x, y)], axis=0
        )
    return (jnp.concatenate([x[0], y[0]], axis=0), low)


def exact_sum(ones, x, dims=NN, left=True):
    high = x.astype(BF16)
    rest = x - high.astype(F32)
    mid = rest.astype(BF16)
    low = (rest - mid.astype(F32)).astype(BF16)
    parts = [dot(ones, z, dims) if left else dot(z, ones, dims) for z in (low, mid, high)]
    return parts[0] + parts[1] + parts[2]


def iotas(rows, columns):
    return (
        lax.broadcasted_iota(jnp.int32, (rows, columns), 0),
        lax.broadcasted_iota(jnp.int32, (rows, columns), 1),
    )


def lane_masks():
    lane = lax.broadcasted_iota(jnp.int32, (1, LANES), 1)
    first = (lane < HS).astype(F32)
    return (first.astype(BF16), (1.0 - first).astype(BF16))


def own_lanes(x0, x1):
    lane = lax.broadcasted_iota(jnp.int32, x0.shape, 1)
    return jnp.where(lane % LANES < HS, x0, x1)


def same_head():
    row, column = iotas(LANES, LANES)
    return row // HS == column // HS


def prepare(r_ref, d_ref, k_ref, x_ref, rate_ref):
    row, column = iotas(ROWS, ROWS)
    sig = jax.nn.sigmoid(d_ref[...].astype(F32))
    log_decay = -DECAY_SCALE * sig
    cum = exact_sum((row >= column).astype(F32).astype(BF16), log_decay)
    x = x_ref[...].astype(F32)
    ones = same_head().astype(F32).astype(BF16)
    inv = lax.rsqrt(exact_sum(ones, x * x, left=False) + 1e-06)
    direction = x * inv
    rate = rate_ref[...].astype(F32)
    ec, ep, en = jnp.exp(cum), jnp.exp(cum - log_decay), jnp.exp(-cum)
    take = -direction * ep
    query = r_ref[...].astype(F32) * ec
    give = direction * rate * en
    key = k_ref[...].astype(F32) * en
    return sig, inv, direction, rate, ec, ep, en, take, query, give, key, ones


def invert(lowers):
    row, column = iotas(ROWS, ROWS)
    eye = (row == column).astype(F32)
    results = [
        eye + jnp.where((row // 2 == column // 2), lower, 0.0) for lower in lowers
    ]
    size = 2
    while size < ROWS:
        here = (row // (2 * size) == column // (2 * size)) & (row // size != column // size)
        splits = [split(x) for x in results]
        offs = [split(jnp.where(here, lower, 0.0)) for lower in lowers]
        halves = [split(mm(x, off)) for x, off in zip(splits, offs)]
        results = [x + mm(h, s) for x, h, s in zip(results, halves, splits)]
        size *= 2
    return results


def compact(x):
    x = jnp.where(same_head(), x, 0.0)
    return x[:HS] + x[HS:]


def expand(x):
    return jnp.where(same_head(), jnp.concatenate([x, x], axis=0), 0.0)


def local_kernel(
    r_ref, d_ref, k_ref, v_ref, x_ref, rate_ref, g_ref,
    send_ref, u_ref, y_ref, w_ref, xx_ref, dv_ref, rr_ref,
):
    _, _, _, _, ec, _, _, take, query, give, key, _ = prepare(
        r_ref, d_ref, k_ref, x_ref, rate_ref
    )
    row, column = iotas(2 * ROWS, 2 * ROWS)
    t_in, s_in = row % ROWS, column % ROWS
    lower = t_in - s_in >= jnp.where(row < ROWS, 1, 0)
    upper = s_in - t_in >= jnp.where(column < ROWS, 1, 0)
    values, grads = (v_ref[...], None), (g_ref[...], None)
    take_s, query_s, give_s, key_s = split(take), split(query), split(give), split(key)
    aq, gk = stack(take_s, query_s), stack(give_s, key_s)
    masks = lane_masks()
    forward = [jnp.where(lower, mm(masked(aq, m), gk, NT), 0.0) for m in masks]
    backward = [split(jnp.where(upper, mm(masked(gk, m), aq, NT), 0.0)) for m in masks]
    inverses = invert([f[:ROWS, :ROWS] for f in forward])
    bv = own_lanes(*[mm(split(f[:ROWS, ROWS:]), values) for f in forward])
    ptg = own_lanes(
        *[mm((b[0][:, ROWS:], b[1][:, ROWS:]), grads) for b in backward]
    )
    bv_s, ptg_s = split(bv), split(ptg[:ROWS])

    def beside(x, y):
        return tuple(jnp.concatenate([p, q], axis=1) for p, q in zip(x, y))

    yu = own_lanes(*[mm(split(m), beside(take_s, bv_s)) for m in inverses])
    xw = own_lanes(*[mm(split(m.T), beside(give_s, ptg_s)) for m in inverses])
    y_ref[...] = yu[:, :LANES]
    u_ref[...] = yu[:, LANES:]
    xx_ref[...] = xw[:, :LANES]
    w_ref[...] = xw[:, LANES:]
    xw_s = split(xw)
    bt = own_lanes(
        *[mm((b[0][ROWS:, :ROWS], b[1][ROWS:, :ROWS]), xw_s) for b in backward]
    )
    rr_ref[...] = bt[:, :LANES] + key
    dv_ref[...] = ptg[ROWS:] + bt[:, LANES:]
    yu_s = split(yu)
    last = ec[ROWS - 1 :, :]
    r128, c128 = iotas(LANES, LANES)
    eye = (r128 == c128).astype(F32)
    y_s = tuple(p[:, :LANES] for p in yu_s)
    u_s = tuple(p[:, LANES:] for p in yu_s)
    w_s = tuple(p[:, LANES:] for p in xw_s)
    send_ref[0, 0] = compact((eye + mm(y_s, give_s, TN)) * last)
    send_ref[0, 1] = compact((mm(u_s, give_s, TN) + mm(values, key_s, TN)) * last)
    send_ref[0, 2] = compact(mm(grads, query_s, TN) + mm(w_s, take_s, TN))


def scan_kernel(
    n, pairs, own_ref, start_ref, end_ref,
    got, starts, ends, sent_sem, got_sem, s_sent, s_got, d_sent, d_got,
):
    me = lax.axis_index("ctx")
    barrier = pltpu.get_barrier_semaphore()
    for j in range(1, n):
        pl.semaphore_signal(
            barrier, inc=1, device_id={"ctx": lax.rem(me + j, n)}, device_id_type=MESH
        )
    pl.semaphore_wait(barrier, n - 1)

    def collect(source, owner):
        return pltpu.make_async_remote_copy(
            src_ref=own_ref.at[owner],
            dst_ref=got.at[source],
            send_sem=sent_sem.at[owner],
            recv_sem=got_sem.at[source],
            device_id={"ctx": owner},
            device_id_type=MESH,
        )

    def give_back(held, target_ref, sent, received, target, owner):
        return pltpu.make_async_remote_copy(
            src_ref=held.at[target],
            dst_ref=target_ref.at[owner],
            send_sem=sent.at[target],
            recv_sem=received.at[owner],
            device_id={"ctx": target},
            device_id_type=MESH,
        )

    def send(j, carry):
        owner = lax.rem(me + j, pairs)

        @pl.when(owner != me)
        def _():
            collect(me, owner).start()

        return carry

    lax.fori_loop(0, pairs, send, 0)

    def scan():
        got[me] = own_ref[me]

        def step(i, carry):
            state, adjoint = carry
            back = n - 1 - i

            @pl.when(i < n // 2)
            def _():
                for source in (i, back):
                    @pl.when(source != me)
                    def _():
                        collect(source, me).wait_recv()

            starts[i] = state
            ends[back] = adjoint
            start_copy = give_back(starts, start_ref, s_sent, s_got, i, me)
            end_copy = give_back(ends, end_ref, d_sent, d_got, back, me)

            @pl.when(i != me)
            def _():
                start_copy.start()

            @pl.when(back != me)
            def _():
                end_copy.start()

            moved = mm(split(state), split(expand(got[i, 0]))) + got[i, 1]
            moved_back = (
                mm(split(adjoint), split(expand(got[back, 0])), NT) + got[back, 2]
            )
            return moved, moved_back

        zero = jnp.zeros((HS, LANES), F32)
        lax.fori_loop(0, n, step, (zero, zero))
        start_ref[me] = starts[me]
        end_ref[me] = ends[me]

        def drain(i, carry):
            @pl.when(i != me)
            def _():
                give_back(starts, start_ref, s_sent, s_got, i, me).wait_send()
                give_back(ends, end_ref, d_sent, d_got, i, me).wait_send()

            return carry

        lax.fori_loop(0, n, drain, 0)

    if n == pairs:
        scan()
    else:
        pl.when(me < pairs)(scan)

    def finish(owner, carry):
        @pl.when(owner != me)
        def _():
            collect(me, owner).wait_send()
            give_back(starts, start_ref, s_sent, s_got, me, owner).wait_recv()
            give_back(ends, end_ref, d_sent, d_got, me, owner).wait_recv()

        return carry

    lax.fori_loop(0, pairs, finish, 0)


def grad_kernel(
    r_ref, d_ref, k_ref, v_ref, x_ref, rate_ref, g_ref,
    start_ref, end_ref, u_ref, y_ref, w_ref, xx_ref, dv_ref, rr_ref,
    gr_ref, gd_ref, gk_ref, gv_ref, gx_ref, grate_ref,
):
    sig, inv, direction, rate, ec, ep, en, take, query, give, key, ones = prepare(
        r_ref, d_ref, k_ref, x_ref, rate_ref
    )
    row, column = iotas(2 * ROWS, 2 * ROWS)
    t_in, s_in = row % ROWS, column % ROWS
    lower = t_in - s_in >= jnp.where(row < ROWS, 0, 1)
    upper = s_in - t_in >= jnp.where(column < ROWS, 0, 1)
    values, grads = (v_ref[...], None), (g_ref[...], None)
    start = expand(start_ref[0])
    after = expand(end_ref[0] * ec[ROWS - 1 :, :])
    start_s, after_s = split(start), split(after)
    u = u_ref[...] + mm(split(y_ref[...]), start_s, NT)
    w = w_ref[...] + mm(split(xx_ref[...]), after_s, NT)
    dv = dv_ref[...] + mm(split(rr_ref[...]), after_s, NT)
    gv_ref[...] = dv.astype(BF16)
    gw, uv = stack(grads, split(w)), stack(split(u), values)
    qa, gk = stack(split(query), split(take)), stack(split(give), split(key))
    masks = lane_masks()
    forward = [split(jnp.where(lower, mm(masked(gw, m), uv, NT), 0.0)) for m in masks]
    backward = [split(jnp.where(upper, mm(masked(uv, m), gw, NT), 0.0)) for m in masks]
    uvd = mm(uv, after_s)
    dqa = mm(gw, start_s) + own_lanes(*[mm(f, gk) for f in forward])
    dgk = uvd + own_lanes(*[mm(b, qa) for b in backward])
    dq, da, dg, dk = dqa[:ROWS], dqa[ROWS:], dgk[:ROWS], dgk[ROWS:]
    gr_ref[...] = (dq * ec).astype(BF16)
    gk_ref[...] = (dk * en).astype(BF16)
    dg_plain = dg * en
    grate_ref[...] = (dg_plain * direction).astype(BF16)
    d_dir = dg_plain * rate - da * ep
    along = exact_sum(ones, direction * d_dir, left=False)
    gx_ref[...] = (inv * (d_dir - direction * along)).astype(BF16)
    d_previous = take * da
    d_cum = query * dq - give * dg - key * dk + d_previous
    at_end = (
        jnp.sum(start * after, axis=0, keepdims=True)
        + jnp.sum(give * uvd[:ROWS] + key * uvd[ROWS:], axis=0, keepdims=True)
    )
    r128, c128 = iotas(ROWS, ROWS)
    d_log = exact_sum((r128 <= c128).astype(F32).astype(BF16), d_cum) - d_previous + at_end
    gd_ref[...] = (d_log * (-DECAY_SCALE) * sig * (1.0 - sig)).astype(BF16)


def per_device(*arrays):
    rows, width = arrays[0].shape
    pairs = width // LANES
    n = lax.axis_size("ctx")
    tokens = pl.BlockSpec((rows, LANES), lambda i: (0, i))
    wide = jax.ShapeDtypeStruct((rows, width), F32)
    params = pltpu.CompilerParams(vmem_limit_bytes=48 * 1024 * 1024)
    local = pl.pallas_call(
        local_kernel,
        grid=(pairs,),
        in_specs=[tokens] * 7,
        out_specs=[pl.BlockSpec((1, 3, HS, LANES), lambda i: (i, 0, 0, 0))] + [tokens] * 6,
        out_shape=[jax.ShapeDtypeStruct((pairs, 3, HS, LANES), F32)] + [wide] * 6,
        compiler_params=params,
    )(*arrays)
    state = jax.ShapeDtypeStruct((pairs, HS, LANES), F32)
    vmem = pl.BlockSpec(memory_space=pltpu.VMEM)
    start, end = pl.pallas_call(
        functools.partial(scan_kernel, n, pairs),
        in_specs=[vmem],
        out_specs=[vmem, vmem],
        out_shape=[state, state],
        scratch_shapes=[
            pltpu.VMEM((n, 3, HS, LANES), F32),
            pltpu.VMEM((n, HS, LANES), F32),
            pltpu.VMEM((n, HS, LANES), F32),
            pltpu.SemaphoreType.DMA((pairs,)),
            pltpu.SemaphoreType.DMA((n,)),
            pltpu.SemaphoreType.DMA((n,)),
            pltpu.SemaphoreType.DMA((pairs,)),
            pltpu.SemaphoreType.DMA((n,)),
            pltpu.SemaphoreType.DMA((pairs,)),
        ],
        compiler_params=pltpu.CompilerParams(
            collective_id=0, has_side_effects=True, vmem_limit_bytes=48 * 1024 * 1024
        ),
    )(local[0])
    one = pl.BlockSpec((1, HS, LANES), lambda i: (i, 0, 0))
    return tuple(
        pl.pallas_call(
            grad_kernel,
            grid=(pairs,),
            in_specs=[tokens] * 7 + [one, one] + [tokens] * 6,
            out_specs=[tokens] * 6,
            out_shape=[jax.ShapeDtypeStruct((rows, width), BF16)] * 6,
            compiler_params=params,
        )(*arrays, start, end, *local[1:])
    )


def solution(mesh):
    placed = P(("groups", "ctx"), None)
    return jax.shard_map(
        per_device,
        mesh=mesh,
        in_specs=(placed,) * 7,
        out_specs=(placed,) * 6,
        check_vma=False,
    )
```

```python
import functools

import jax
import jax.numpy as jnp
from jax import lax
from jax.experimental import pallas as pl
from jax.experimental.pallas import tpu as pltpu
from jax.sharding import PartitionSpec as P

HS = 64
LANES = 128
ROWS = 128
LOCAL = 4
LATER = 4
DECAY_SCALE = 0.6065306597126334
MESH = pl.DeviceIdType.MESH
NN = (((1,), (0,)), ((), ()))
NT = (((1,), (1,)), ((), ()))
TN = (((0,), (0,)), ((), ()))
F32 = jnp.float32
BF16 = jnp.bfloat16


def dot(x, y, dims):
    return lax.dot_general(x, y, dims, preferred_element_type=F32)


def split(x):
    if x.dtype == BF16:
        return (x, None)
    high = x.astype(BF16)
    return (high, (x - high.astype(F32)).astype(BF16))


def mm(x, y, dims=NN):
    total = dot(x[0], y[0], dims)
    if y[1] is not None:
        total = total + dot(x[0], y[1], dims)
    if x[1] is not None:
        total = total + dot(x[1], y[0], dims)
    return total


def masked(x, mask):
    return tuple(None if part is None else part * mask for part in x)


def stack(x, y):
    low = None
    if x[1] is not None or y[1] is not None:
        low = jnp.concatenate(
            [jnp.zeros_like(z[0]) if z[1] is None else z[1] for z in (x, y)], axis=0
        )
    return (jnp.concatenate([x[0], y[0]], axis=0), low)


def exact_sum(ones, x, dims=NN, left=True):
    high = x.astype(BF16)
    rest = x - high.astype(F32)
    mid = rest.astype(BF16)
    low = (rest - mid.astype(F32)).astype(BF16)
    parts = [dot(ones, z, dims) if left else dot(z, ones, dims) for z in (low, mid, high)]
    return parts[0] + parts[1] + parts[2]


def iotas(rows, columns):
    return (
        lax.broadcasted_iota(jnp.int32, (rows, columns), 0),
        lax.broadcasted_iota(jnp.int32, (rows, columns), 1),
    )


def lane_masks():
    lane = lax.broadcasted_iota(jnp.int32, (1, LANES), 1)
    first = (lane < HS).astype(F32)
    return (first.astype(BF16), (1.0 - first).astype(BF16))


def own_lanes(x0, x1):
    lane = lax.broadcasted_iota(jnp.int32, x0.shape, 1)
    return jnp.where(lane % LANES < HS, x0, x1)


def same_head():
    row, column = iotas(LANES, LANES)
    return row // HS == column // HS


def prepare(r_ref, d_ref, k_ref, x_ref, rate_ref):
    row, column = iotas(ROWS, ROWS)
    sig = jax.nn.sigmoid(d_ref[...].astype(F32))
    log_decay = -DECAY_SCALE * sig
    cum = exact_sum((row >= column).astype(F32).astype(BF16), log_decay)
    x = x_ref[...].astype(F32)
    ones = same_head().astype(F32).astype(BF16)
    inv = lax.rsqrt(exact_sum(ones, x * x, left=False) + 1e-06)
    direction = x * inv
    rate = rate_ref[...].astype(F32)
    ec, ep, en = jnp.exp(cum), jnp.exp(cum - log_decay), jnp.exp(-cum)
    take = -direction * ep
    query = r_ref[...].astype(F32) * ec
    give = direction * rate * en
    key = k_ref[...].astype(F32) * en
    return sig, inv, direction, rate, ec, ep, en, take, query, give, key, ones


def invert(lowers):
    row, column = iotas(ROWS, ROWS)
    eye = (row == column).astype(F32)
    results = [
        eye + jnp.where((row // 2 == column // 2), lower, 0.0) for lower in lowers
    ]
    size = 2
    while size < ROWS:
        here = (row // (2 * size) == column // (2 * size)) & (row // size != column // size)
        splits = [split(x) for x in results]
        offs = [split(jnp.where(here, lower, 0.0)) for lower in lowers]
        halves = [split(mm(x, off)) for x, off in zip(splits, offs)]
        results = [x + mm(h, s) for x, h, s in zip(results, halves, splits)]
        size *= 2
    return results


def compact(x):
    x = jnp.where(same_head(), x, 0.0)
    return x[:HS] + x[HS:]


def expand(x):
    return jnp.where(same_head(), jnp.concatenate([x, x], axis=0), 0.0)


def beside(x, y):
    return tuple(jnp.concatenate([p, q], axis=1) for p, q in zip(x, y))


def local_first(r_ref, d_ref, k_ref, v_ref, x_ref, rate_ref, g_ref):
    _, _, _, _, ec, _, _, take, query, give, key, _ = prepare(
        r_ref, d_ref, k_ref, x_ref, rate_ref
    )
    row, column = iotas(2 * ROWS, 2 * ROWS)
    t_in, s_in = row % ROWS, column % ROWS
    lower = t_in - s_in >= jnp.where(row < ROWS, 1, 0)
    upper = s_in - t_in >= jnp.where(column < ROWS, 1, 0)
    values, grads = (v_ref[...], None), (g_ref[...], None)
    take_s, query_s, give_s, key_s = split(take), split(query), split(give), split(key)
    aq, gk = stack(take_s, query_s), stack(give_s, key_s)
    masks = lane_masks()
    forward = [
        jnp.where(lower[:ROWS], mm(masked(take_s, m), gk, NT), 0.0) for m in masks
    ]
    backward = [split(jnp.where(upper, mm(masked(gk, m), aq, NT), 0.0)) for m in masks]
    bv = own_lanes(*[mm(split(f[:, ROWS:]), values) for f in forward])
    ptg = own_lanes(
        *[mm((b[0][:, ROWS:], b[1][:, ROWS:]), grads) for b in backward]
    )
    lowers = [f[:, :ROWS] for f in forward]
    take_bv = beside(take_s, split(bv))
    give_ptg = beside(give_s, split(ptg[:ROWS]))
    bts = [(b[0][ROWS:, :ROWS], b[1][ROWS:, :ROWS]) for b in backward]
    return lowers, (
        take_bv, give_ptg, bts, ptg[ROWS:], key, values, grads,
        take_s, query_s, give_s, key_s, ec[ROWS - 1 :, :],
    )


def local_second(inverses, kept, at, send_ref, u_ref, y_ref, w_ref, xx_ref, dv_ref, rr_ref):
    (
        take_bv, give_ptg, bts, qtg, key, values, grads,
        take_s, query_s, give_s, key_s, last,
    ) = kept
    lanes = slice(at * LANES, (at + 1) * LANES)
    yu = own_lanes(*[mm(split(m), take_bv) for m in inverses])
    xw = own_lanes(*[mm(split(m.T), give_ptg) for m in inverses])
    y_ref[:, lanes] = yu[:, :LANES]
    u_ref[:, lanes] = yu[:, LANES:]
    xx_ref[:, lanes] = xw[:, :LANES]
    w_ref[:, lanes] = xw[:, LANES:]
    xw_s = split(xw)
    bt = own_lanes(*[mm(b, xw_s) for b in bts])
    rr_ref[:, lanes] = bt[:, :LANES] + key
    dv_ref[:, lanes] = qtg + bt[:, LANES:]
    yu_s = split(yu)
    r128, c128 = iotas(LANES, LANES)
    eye = (r128 == c128).astype(F32)
    y_s = tuple(p[:, :LANES] for p in yu_s)
    u_s = tuple(p[:, LANES:] for p in yu_s)
    w_s = tuple(p[:, LANES:] for p in xw_s)
    send_ref[at, 0] = compact((eye + mm(y_s, give_s, TN)) * last)
    send_ref[at, 1] = compact((mm(u_s, give_s, TN) + mm(values, key_s, TN)) * last)
    send_ref[at, 2] = compact(mm(grads, query_s, TN) + mm(w_s, take_s, TN))


def lanes_of(refs, at):
    return [ref.at[:, at * LANES : (at + 1) * LANES] for ref in refs]


def local_kernel(*refs):
    count = refs[0].shape[1] // LANES
    firsts = [local_first(*lanes_of(refs[:7], at)) for at in range(count)]
    inverses = invert([x for lowers, _ in firsts for x in lowers])
    for at, (_, kept) in enumerate(firsts):
        local_second(inverses[2 * at : 2 * at + 2], kept, at, *refs[7:])


def scan_kernel(
    n, pairs, own_ref, start_ref, end_ref,
    got, starts, ends, sent_sem, got_sem, s_sent, s_got, d_sent, d_got,
):
    me = lax.axis_index("ctx")
    barrier = pltpu.get_barrier_semaphore()
    for j in range(1, n):
        pl.semaphore_signal(
            barrier, inc=1, device_id={"ctx": lax.rem(me + j, n)}, device_id_type=MESH
        )
    pl.semaphore_wait(barrier, n - 1)

    def collect(source, owner):
        return pltpu.make_async_remote_copy(
            src_ref=own_ref.at[owner],
            dst_ref=got.at[source],
            send_sem=sent_sem.at[owner],
            recv_sem=got_sem.at[source],
            device_id={"ctx": owner},
            device_id_type=MESH,
        )

    def give_back(held, target_ref, sent, received, target, owner):
        return pltpu.make_async_remote_copy(
            src_ref=held.at[target],
            dst_ref=target_ref.at[owner],
            send_sem=sent.at[target],
            recv_sem=received.at[owner],
            device_id={"ctx": target},
            device_id_type=MESH,
        )

    def send(j, carry):
        owner = lax.rem(me + j, pairs)

        @pl.when(owner != me)
        def _():
            collect(me, owner).start()

        return carry

    lax.fori_loop(0, pairs, send, 0)

    def scan():
        got[me] = own_ref[me]

        def step(i, carry):
            state, adjoint = carry
            back = n - 1 - i

            @pl.when(i < n // 2)
            def _():
                for source in (i, back):
                    @pl.when(source != me)
                    def _():
                        collect(source, me).wait_recv()

            starts[i] = state
            ends[back] = adjoint
            start_copy = give_back(starts, start_ref, s_sent, s_got, i, me)
            end_copy = give_back(ends, end_ref, d_sent, d_got, back, me)

            @pl.when(i != me)
            def _():
                start_copy.start()

            @pl.when(back != me)
            def _():
                end_copy.start()

            moved = mm(split(state), split(expand(got[i, 0]))) + got[i, 1]
            moved_back = (
                mm(split(adjoint), split(expand(got[back, 0])), NT) + got[back, 2]
            )
            return moved, moved_back

        zero = jnp.zeros((HS, LANES), F32)
        lax.fori_loop(0, n, step, (zero, zero))
        start_ref[me] = starts[me]
        end_ref[me] = ends[me]

        def drain(i, carry):
            @pl.when(i != me)
            def _():
                give_back(starts, start_ref, s_sent, s_got, i, me).wait_send()
                give_back(ends, end_ref, d_sent, d_got, i, me).wait_send()

            return carry

        lax.fori_loop(0, n, drain, 0)

    if n == pairs:
        scan()
    else:
        pl.when(me < pairs)(scan)

    def finish(owner, carry):
        @pl.when(owner != me)
        def _():
            collect(me, owner).wait_send()
            give_back(starts, start_ref, s_sent, s_got, me, owner).wait_recv()
            give_back(ends, end_ref, d_sent, d_got, me, owner).wait_recv()

        return carry

    lax.fori_loop(0, pairs, finish, 0)


def grad_kernel(
    r_ref, d_ref, k_ref, v_ref, x_ref, rate_ref, g_ref,
    start_ref, end_ref, u_ref, y_ref, w_ref, xx_ref, dv_ref, rr_ref,
    gr_ref, gd_ref, gk_ref, gv_ref, gx_ref, grate_ref,
):
    sig, inv, direction, rate, ec, ep, en, take, query, give, key, ones = prepare(
        r_ref, d_ref, k_ref, x_ref, rate_ref
    )
    row, column = iotas(2 * ROWS, 2 * ROWS)
    t_in, s_in = row % ROWS, column % ROWS
    lower = t_in - s_in >= jnp.where(row < ROWS, 0, 1)
    upper = s_in - t_in >= jnp.where(column < ROWS, 0, 1)
    values, grads = (v_ref[...], None), (g_ref[...], None)
    start = expand(start_ref[0])
    after = expand(end_ref[0] * ec[ROWS - 1 :, :])
    start_s, after_s = split(start), split(after)
    u = u_ref[...] + mm(split(y_ref[...]), start_s, NT)
    w = w_ref[...] + mm(split(xx_ref[...]), after_s, NT)
    dv = dv_ref[...] + mm(split(rr_ref[...]), after_s, NT)
    gv_ref[...] = dv.astype(BF16)
    gw, uv = stack(grads, split(w)), stack(split(u), values)
    qa, gk = stack(split(query), split(take)), stack(split(give), split(key))
    masks = lane_masks()
    forward = [split(jnp.where(lower, mm(masked(gw, m), uv, NT), 0.0)) for m in masks]
    backward = [split(jnp.where(upper, mm(masked(uv, m), gw, NT), 0.0)) for m in masks]
    uvd = mm(uv, after_s)
    dqa = mm(gw, start_s) + own_lanes(*[mm(f, gk) for f in forward])
    dgk = uvd + own_lanes(*[mm(b, qa) for b in backward])
    dq, da, dg, dk = dqa[:ROWS], dqa[ROWS:], dgk[:ROWS], dgk[ROWS:]
    gr_ref[...] = (dq * ec).astype(BF16)
    gk_ref[...] = (dk * en).astype(BF16)
    dg_plain = dg * en
    grate_ref[...] = (dg_plain * direction).astype(BF16)
    d_dir = dg_plain * rate - da * ep
    along = exact_sum(ones, direction * d_dir, left=False)
    gx_ref[...] = (inv * (d_dir - direction * along)).astype(BF16)
    d_previous = take * da
    d_cum = query * dq - give * dg - key * dk + d_previous
    at_end = (
        jnp.sum(start * after, axis=0, keepdims=True)
        + jnp.sum(give * uvd[:ROWS] + key * uvd[ROWS:], axis=0, keepdims=True)
    )
    r128, c128 = iotas(ROWS, ROWS)
    d_log = exact_sum((r128 <= c128).astype(F32).astype(BF16), d_cum) - d_previous + at_end
    gd_ref[...] = (d_log * (-DECAY_SCALE) * sig * (1.0 - sig)).astype(BF16)


def grads_kernel(*refs):
    for at in range(refs[0].shape[1] // LANES):
        one = [ref.at[at : at + 1] for ref in refs[7:9]]
        grad_kernel(*lanes_of(refs[:7], at), *one, *lanes_of(refs[9:], at))


def per_device(*arrays):
    rows, width = arrays[0].shape
    pairs = width // LANES
    n = lax.axis_size("ctx")
    tokens = pl.BlockSpec((rows, LOCAL * LANES), lambda i: (0, i))
    later = pl.BlockSpec((rows, LATER * LANES), lambda i: (0, i))
    wide = jax.ShapeDtypeStruct((rows, width), F32)
    params = pltpu.CompilerParams(vmem_limit_bytes=60 * 1024 * 1024)
    local = pl.pallas_call(
        local_kernel,
        grid=(pairs // LOCAL,),
        in_specs=[tokens] * 7,
        out_specs=[pl.BlockSpec((LOCAL, 3, HS, LANES), lambda i: (i, 0, 0, 0))] + [tokens] * 6,
        out_shape=[jax.ShapeDtypeStruct((pairs, 3, HS, LANES), F32)] + [wide] * 6,
        compiler_params=params,
    )(*arrays)
    state = jax.ShapeDtypeStruct((pairs, HS, LANES), F32)
    vmem = pl.BlockSpec(memory_space=pltpu.VMEM)
    start, end = pl.pallas_call(
        functools.partial(scan_kernel, n, pairs),
        in_specs=[vmem],
        out_specs=[vmem, vmem],
        out_shape=[state, state],
        scratch_shapes=[
            pltpu.VMEM((n, 3, HS, LANES), F32),
            pltpu.VMEM((n, HS, LANES), F32),
            pltpu.VMEM((n, HS, LANES), F32),
            pltpu.SemaphoreType.DMA((pairs,)),
            pltpu.SemaphoreType.DMA((n,)),
            pltpu.SemaphoreType.DMA((n,)),
            pltpu.SemaphoreType.DMA((pairs,)),
            pltpu.SemaphoreType.DMA((n,)),
            pltpu.SemaphoreType.DMA((pairs,)),
        ],
        compiler_params=pltpu.CompilerParams(
            collective_id=0, has_side_effects=True, vmem_limit_bytes=48 * 1024 * 1024
        ),
    )(local[0])
    one = pl.BlockSpec((LATER, HS, LANES), lambda i: (i, 0, 0))
    return tuple(
        pl.pallas_call(
            grads_kernel,
            grid=(pairs // LATER,),
            in_specs=[later] * 7 + [one, one] + [later] * 6,
            out_specs=[later] * 6,
            out_shape=[jax.ShapeDtypeStruct((rows, width), BF16)] * 6,
            compiler_params=params,
        )(*arrays, start, end, *local[1:])
    )


def solution(mesh):
    placed = P(("groups", "ctx"), None)
    return jax.shard_map(
        per_device,
        mesh=mesh,
        in_specs=(placed,) * 7,
        out_specs=(placed,) * 6,
        check_vma=False,
    )
```

```python
import functools

import jax
import jax.numpy as jnp
from jax import lax
from jax.experimental import pallas as pl
from jax.experimental.pallas import tpu as pltpu
from jax.sharding import PartitionSpec as P

HS = 64
LANES = 128
ROWS = 128
LOCAL = 4
LATER = 4
DECAY_SCALE = 0.6065306597126334
MESH = pl.DeviceIdType.MESH
NN = (((1,), (0,)), ((), ()))
NT = (((1,), (1,)), ((), ()))
TN = (((0,), (0,)), ((), ()))
F32 = jnp.float32
BF16 = jnp.bfloat16


def dot(x, y, dims):
    return lax.dot_general(x, y, dims, preferred_element_type=F32)


def split(x):
    if x.dtype == BF16:
        return (x, None)
    high = x.astype(BF16)
    return (high, (x - high.astype(F32)).astype(BF16))


def mm(x, y, dims=NN):
    total = dot(x[0], y[0], dims)
    if y[1] is not None:
        total = total + dot(x[0], y[1], dims)
    if x[1] is not None:
        total = total + dot(x[1], y[0], dims)
    return total


def masked(x, mask):
    return tuple(None if part is None else part * mask for part in x)


def stack(x, y):
    low = None
    if x[1] is not None or y[1] is not None:
        low = jnp.concatenate(
            [jnp.zeros_like(z[0]) if z[1] is None else z[1] for z in (x, y)], axis=0
        )
    return (jnp.concatenate([x[0], y[0]], axis=0), low)


def exact_sum(ones, x, dims=NN, left=True):
    high = x.astype(BF16)
    rest = x - high.astype(F32)
    mid = rest.astype(BF16)
    low = (rest - mid.astype(F32)).astype(BF16)
    parts = [dot(ones, z, dims) if left else dot(z, ones, dims) for z in (low, mid, high)]
    return parts[0] + parts[1] + parts[2]


def iotas(rows, columns):
    return (
        lax.broadcasted_iota(jnp.int32, (rows, columns), 0),
        lax.broadcasted_iota(jnp.int32, (rows, columns), 1),
    )


def lane_masks():
    lane = lax.broadcasted_iota(jnp.int32, (1, LANES), 1)
    first = (lane < HS).astype(F32)
    return (first.astype(BF16), (1.0 - first).astype(BF16))


def own_lanes(x0, x1):
    lane = lax.broadcasted_iota(jnp.int32, x0.shape, 1)
    return jnp.where(lane % LANES < HS, x0, x1)


def same_head():
    row, column = iotas(LANES, LANES)
    return row // HS == column // HS


def prepare(r_ref, d_ref, k_ref, x_ref, rate_ref):
    row, column = iotas(ROWS, ROWS)
    sig = jax.nn.sigmoid(d_ref[...].astype(F32))
    log_decay = -DECAY_SCALE * sig
    cum = exact_sum((row >= column).astype(F32).astype(BF16), log_decay)
    x = x_ref[...].astype(F32)
    ones = same_head().astype(F32).astype(BF16)
    inv = lax.rsqrt(exact_sum(ones, x * x, left=False) + 1e-06)
    direction = x * inv
    rate = rate_ref[...].astype(F32)
    ec, ep, en = jnp.exp(cum), jnp.exp(cum - log_decay), jnp.exp(-cum)
    take = -direction * ep
    query = r_ref[...].astype(F32) * ec
    give = direction * rate * en
    key = k_ref[...].astype(F32) * en
    return sig, inv, direction, rate, ec, ep, en, take, query, give, key, ones


def invert(lowers):
    row, column = iotas(ROWS, ROWS)
    eye = (row == column).astype(F32)
    results = [
        eye + jnp.where((row // 2 == column // 2), lower, 0.0) for lower in lowers
    ]
    size = 2
    while size < ROWS:
        here = (row // (2 * size) == column // (2 * size)) & (row // size != column // size)
        splits = [split(x) for x in results]
        offs = [split(jnp.where(here, lower, 0.0)) for lower in lowers]
        halves = [split(mm(x, off)) for x, off in zip(splits, offs)]
        results = [x + mm(h, s) for x, h, s in zip(results, halves, splits)]
        size *= 2
    return results


def compact(x):
    x = jnp.where(same_head(), x, 0.0)
    return x[:HS] + x[HS:]


def expand(x):
    return jnp.where(same_head(), jnp.concatenate([x, x], axis=0), 0.0)


def beside(x, y):
    return tuple(jnp.concatenate([p, q], axis=1) for p, q in zip(x, y))


def local_first(r_ref, d_ref, k_ref, v_ref, x_ref, rate_ref, g_ref):
    _, _, _, _, ec, _, _, take, query, give, key, _ = prepare(
        r_ref, d_ref, k_ref, x_ref, rate_ref
    )
    row, column = iotas(2 * ROWS, 2 * ROWS)
    t_in, s_in = row % ROWS, column % ROWS
    lower = t_in - s_in >= jnp.where(row < ROWS, 1, 0)
    upper = s_in - t_in >= jnp.where(column < ROWS, 1, 0)
    values, grads = (v_ref[...], None), (g_ref[...], None)
    take_s, query_s, give_s, key_s = split(take), split(query), split(give), split(key)
    aq, gk = stack(take_s, query_s), stack(give_s, key_s)
    masks = lane_masks()
    forward = [
        jnp.where(lower[:ROWS], mm(masked(take_s, m), gk, NT), 0.0) for m in masks
    ]
    backward = [split(jnp.where(upper, mm(masked(gk, m), aq, NT), 0.0)) for m in masks]
    bv = own_lanes(*[mm(split(f[:, ROWS:]), values) for f in forward])
    ptg = own_lanes(
        *[mm((b[0][:, ROWS:], b[1][:, ROWS:]), grads) for b in backward]
    )
    lowers = [f[:, :ROWS] for f in forward]
    take_bv = beside(take_s, split(bv))
    give_ptg = beside(give_s, split(ptg[:ROWS]))
    bts = [(b[0][ROWS:, :ROWS], b[1][ROWS:, :ROWS]) for b in backward]
    return lowers, (
        take_bv, give_ptg, bts, ptg[ROWS:], key, values, grads,
        take_s, query_s, give_s, key_s, ec[ROWS - 1 :, :],
    )


def local_second(inverses, kept, at, send_ref, u_ref, y_ref, w_ref, xx_ref, dv_ref, rr_ref):
    (
        take_bv, give_ptg, bts, qtg, key, values, grads,
        take_s, query_s, give_s, key_s, last,
    ) = kept
    lanes = slice(at * LANES, (at + 1) * LANES)
    yu = own_lanes(*[mm(split(m), take_bv) for m in inverses])
    xw = own_lanes(*[mm(split(m.T), give_ptg) for m in inverses])
    y_ref[:, lanes] = yu[:, :LANES]
    u_ref[:, lanes] = yu[:, LANES:]
    xx_ref[:, lanes] = xw[:, :LANES]
    w_ref[:, lanes] = xw[:, LANES:]
    xw_s = split(xw)
    bt = own_lanes(*[mm(b, xw_s) for b in bts])
    rr_ref[:, lanes] = bt[:, :LANES] + key
    dv_ref[:, lanes] = qtg + bt[:, LANES:]
    yu_s = split(yu)
    r128, c128 = iotas(LANES, LANES)
    eye = (r128 == c128).astype(F32)
    y_s = tuple(p[:, :LANES] for p in yu_s)
    u_s = tuple(p[:, LANES:] for p in yu_s)
    w_s = tuple(p[:, LANES:] for p in xw_s)
    send_ref[at, 0] = compact((eye + mm(y_s, give_s, TN)) * last)
    send_ref[at, 1] = compact((mm(u_s, give_s, TN) + mm(values, key_s, TN)) * last)
    send_ref[at, 2] = compact(mm(grads, query_s, TN) + mm(w_s, take_s, TN))


def lanes_of(refs, at):
    return [ref.at[:, at * LANES : (at + 1) * LANES] for ref in refs]


def local_kernel(*refs):
    count = refs[0].shape[1] // LANES
    firsts = [local_first(*lanes_of(refs[:7], at)) for at in range(count)]
    inverses = invert([x for lowers, _ in firsts for x in lowers])
    for at, (_, kept) in enumerate(firsts):
        local_second(inverses[2 * at : 2 * at + 2], kept, at, *refs[7:])


def scan_kernel(
    n, pairs, own_ref, start_ref, end_ref,
    got, starts, ends, sent_sem, got_sem, s_sent, s_got, d_sent, d_got,
):
    me = lax.axis_index("ctx")
    barrier = pltpu.get_barrier_semaphore()
    for j in range(1, n):
        pl.semaphore_signal(
            barrier, inc=1, device_id={"ctx": lax.rem(me + j, n)}, device_id_type=MESH
        )
    pl.semaphore_wait(barrier, n - 1)

    def collect(source, owner):
        return pltpu.make_async_remote_copy(
            src_ref=own_ref.at[owner],
            dst_ref=got.at[source],
            send_sem=sent_sem.at[owner],
            recv_sem=got_sem.at[source],
            device_id={"ctx": owner},
            device_id_type=MESH,
        )

    def give_back(held, target_ref, sent, received, target, owner):
        return pltpu.make_async_remote_copy(
            src_ref=held.at[target],
            dst_ref=target_ref.at[owner],
            send_sem=sent.at[target],
            recv_sem=received.at[owner],
            device_id={"ctx": target},
            device_id_type=MESH,
        )

    def send(j, carry):
        owner = lax.rem(me + pairs // 2 + j, pairs)

        @pl.when(owner != me)
        def _():
            collect(me, owner).start()

        return carry

    lax.fori_loop(0, pairs, send, 0)

    def scan():
        got[me] = own_ref[me]

        def step(i, carry):
            state, adjoint = carry
            back = n - 1 - i

            @pl.when(i < n // 2)
            def _():
                for source in (i, back):
                    @pl.when(source != me)
                    def _():
                        collect(source, me).wait_recv()

            starts[i] = state
            ends[back] = adjoint
            start_copy = give_back(starts, start_ref, s_sent, s_got, i, me)
            end_copy = give_back(ends, end_ref, d_sent, d_got, back, me)

            @pl.when(i != me)
            def _():
                start_copy.start()

            @pl.when(back != me)
            def _():
                end_copy.start()

            moved = mm(split(state), split(expand(got[i, 0]))) + got[i, 1]
            moved_back = (
                mm(split(adjoint), split(expand(got[back, 0])), NT) + got[back, 2]
            )
            return moved, moved_back

        zero = jnp.zeros((HS, LANES), F32)
        lax.fori_loop(0, n, step, (zero, zero))
        start_ref[me] = starts[me]
        end_ref[me] = ends[me]

        def drain(i, carry):
            @pl.when(i != me)
            def _():
                give_back(starts, start_ref, s_sent, s_got, i, me).wait_send()
                give_back(ends, end_ref, d_sent, d_got, i, me).wait_send()

            return carry

        lax.fori_loop(0, n, drain, 0)

    if n == pairs:
        scan()
    else:
        pl.when(me < pairs)(scan)

    def finish(owner, carry):
        @pl.when(owner != me)
        def _():
            collect(me, owner).wait_send()
            give_back(starts, start_ref, s_sent, s_got, me, owner).wait_recv()
            give_back(ends, end_ref, d_sent, d_got, me, owner).wait_recv()

        return carry

    lax.fori_loop(0, pairs, finish, 0)


def grad_kernel(
    r_ref, d_ref, k_ref, v_ref, x_ref, rate_ref, g_ref,
    start_ref, end_ref, u_ref, y_ref, w_ref, xx_ref, dv_ref, rr_ref,
    gr_ref, gd_ref, gk_ref, gv_ref, gx_ref, grate_ref,
):
    sig, inv, direction, rate, ec, ep, en, take, query, give, key, ones = prepare(
        r_ref, d_ref, k_ref, x_ref, rate_ref
    )
    row, column = iotas(2 * ROWS, 2 * ROWS)
    t_in, s_in = row % ROWS, column % ROWS
    lower = t_in - s_in >= jnp.where(row < ROWS, 0, 1)
    upper = s_in - t_in >= jnp.where(column < ROWS, 0, 1)
    values, grads = (v_ref[...], None), (g_ref[...], None)
    start = expand(start_ref[0])
    after = expand(end_ref[0] * ec[ROWS - 1 :, :])
    start_s, after_s = split(start), split(after)
    u = u_ref[...] + mm(split(y_ref[...]), start_s, NT)
    w = w_ref[...] + mm(split(xx_ref[...]), after_s, NT)
    dv = dv_ref[...] + mm(split(rr_ref[...]), after_s, NT)
    gv_ref[...] = dv.astype(BF16)
    gw, uv = stack(grads, split(w)), stack(split(u), values)
    qa, gk = stack(split(query), split(take)), stack(split(give), split(key))
    masks = lane_masks()
    forward = [split(jnp.where(lower, mm(masked(gw, m), uv, NT), 0.0)) for m in masks]
    backward = [split(jnp.where(upper, mm(masked(uv, m), gw, NT), 0.0)) for m in masks]
    uvd = mm(uv, after_s)
    dqa = mm(gw, start_s) + own_lanes(*[mm(f, gk) for f in forward])
    dgk = uvd + own_lanes(*[mm(b, qa) for b in backward])
    dq, da, dg, dk = dqa[:ROWS], dqa[ROWS:], dgk[:ROWS], dgk[ROWS:]
    gr_ref[...] = (dq * ec).astype(BF16)
    gk_ref[...] = (dk * en).astype(BF16)
    dg_plain = dg * en
    grate_ref[...] = (dg_plain * direction).astype(BF16)
    d_dir = dg_plain * rate - da * ep
    along = exact_sum(ones, direction * d_dir, left=False)
    gx_ref[...] = (inv * (d_dir - direction * along)).astype(BF16)
    d_previous = take * da
    d_cum = query * dq - give * dg - key * dk + d_previous
    at_end = (
        jnp.sum(start * after, axis=0, keepdims=True)
        + jnp.sum(give * uvd[:ROWS] + key * uvd[ROWS:], axis=0, keepdims=True)
    )
    r128, c128 = iotas(ROWS, ROWS)
    d_log = exact_sum((r128 <= c128).astype(F32).astype(BF16), d_cum) - d_previous + at_end
    gd_ref[...] = (d_log * (-DECAY_SCALE) * sig * (1.0 - sig)).astype(BF16)


def grads_kernel(*refs):
    for at in range(refs[0].shape[1] // LANES):
        one = [ref.at[at : at + 1] for ref in refs[7:9]]
        grad_kernel(*lanes_of(refs[:7], at), *one, *lanes_of(refs[9:], at))


def per_device(*arrays):
    rows, width = arrays[0].shape
    pairs = width // LANES
    n = lax.axis_size("ctx")
    tokens = pl.BlockSpec((rows, LOCAL * LANES), lambda i: (0, i))
    later = pl.BlockSpec((rows, LATER * LANES), lambda i: (0, i))
    wide = jax.ShapeDtypeStruct((rows, width), F32)
    params = pltpu.CompilerParams(vmem_limit_bytes=60 * 1024 * 1024)
    local = pl.pallas_call(
        local_kernel,
        grid=(pairs // LOCAL,),
        in_specs=[tokens] * 7,
        out_specs=[pl.BlockSpec((LOCAL, 3, HS, LANES), lambda i: (i, 0, 0, 0))] + [tokens] * 6,
        out_shape=[jax.ShapeDtypeStruct((pairs, 3, HS, LANES), F32)] + [wide] * 6,
        compiler_params=params,
    )(*arrays)
    state = jax.ShapeDtypeStruct((pairs, HS, LANES), F32)
    vmem = pl.BlockSpec(memory_space=pltpu.VMEM)
    start, end = pl.pallas_call(
        functools.partial(scan_kernel, n, pairs),
        in_specs=[vmem],
        out_specs=[vmem, vmem],
        out_shape=[state, state],
        scratch_shapes=[
            pltpu.VMEM((n, 3, HS, LANES), F32),
            pltpu.VMEM((n, HS, LANES), F32),
            pltpu.VMEM((n, HS, LANES), F32),
            pltpu.SemaphoreType.DMA((pairs,)),
            pltpu.SemaphoreType.DMA((n,)),
            pltpu.SemaphoreType.DMA((n,)),
            pltpu.SemaphoreType.DMA((pairs,)),
            pltpu.SemaphoreType.DMA((n,)),
            pltpu.SemaphoreType.DMA((pairs,)),
        ],
        compiler_params=pltpu.CompilerParams(
            collective_id=0, has_side_effects=True, vmem_limit_bytes=48 * 1024 * 1024
        ),
    )(local[0])
    one = pl.BlockSpec((LATER, HS, LANES), lambda i: (i, 0, 0))
    return tuple(
        pl.pallas_call(
            grads_kernel,
            grid=(pairs // LATER,),
            in_specs=[later] * 7 + [one, one] + [later] * 6,
            out_specs=[later] * 6,
            out_shape=[jax.ShapeDtypeStruct((rows, width), BF16)] * 6,
            compiler_params=params,
        )(*arrays, start, end, *local[1:])
    )


def solution(mesh):
    placed = P(("groups", "ctx"), None)
    return jax.shard_map(
        per_device,
        mesh=mesh,
        in_specs=(placed,) * 7,
        out_specs=(placed,) * 6,
        check_vma=False,
    )
```
